32 devices in a mesh: ta: 2 (over core), ha: 4 (over y, x), wa: 4 (over z).
Axes of the slice: x: 2, y: 2, z: 4, core: 2. Of those that a mesh axis runs over, the one named last changes fastest.
Arguments:
- queries: bfloat16 [2, 4, 4, 24, 1536], P('ta', 'ha', 'wa'), may hold values from -6 to 6
- current_kv: bfloat16 [2, 4, 4, 2, 24, 1536], P('ta', 'ha', 'wa'), may hold values from -18 to 18
- stale_kv: bfloat16 [2, 4, 4, 2, 24, 1536], P('ta', 'ha', 'wa'), may hold values from -18 to 18
- text_kv: bfloat16 [2, 16, 1536], P(None, 'wa'), may hold values from -18 to 18
- q_gain: float32 [128], replicated, may hold values from 0.8 to 1.8
- k_gain: float32 [128], replicated, may hold values from 0.8 to 1.8
- pattern: int32 [2, 4, 4, 27], P('ta', 'ha', 'wa'), may hold values 0 or 1
Outputs:
- attended: bfloat16 [2, 4, 4, 24, 1536], P('ta', 'ha', 'wa')
The draws below stay inside these ranges and needn't reach their ends.
Inputs may be any that keep to these rules, and one draw needn't show every extreme that they name: pattern holds 0 or 1; its entry 13 and entries pointing out of the grid are not read.
All inputs are finite; a program needn't handle non-finite values. No bound on the sum of `pattern` on one device may be relied on, other than what follows from the above.
Results may differ from the reference program's by a relative error of at most 0.0082.
Values may be sent and summed in bfloat16 or wider, within the bound.
No kernel may reach another device: no remote copies, remote signals or barrier semaphores. Data moves between devices by JAX's collectives and lax.ppermute only.
A program may use at most 64 MiB of HBM per device.

```python
import math
import jax
import jax.numpy as jnp
import numpy as np
from jax import lax

HD = 128
HEADS = 12
TILE = 24
OFFSETS = 27
F = 1536
TEXT = 16
N_TA = 2
N_HA = 4
N_WA = 4


def touch_ends(values, key, least, top_value):
    shape = values.shape
    index_at = [jax.random.randint(jax.random.fold_in(key, axis), (), 0, shape[axis]) for axis in range(len(shape))]
    values = values.at[tuple(index_at)].set(least)
    longest = shape.index(max(shape))
    index_at[longest] = (index_at[longest] + 1) % shape[longest]
    return values.at[tuple(index_at)].set(top_value)


def levels(own_key, shape, pieces, low, largest):
    def one(dim, blocks):
        steps = jax.random.uniform(jax.random.fold_in(jax.random.fold_in(own_key, 6), dim), (blocks,), jnp.float32, low / len(pieces), largest / len(pieces))
        return jnp.repeat(jnp.exp(steps), shape[dim] // blocks).reshape((-1,) + (1,) * (len(shape) - dim - 1))

    level = one(*pieces[0])
    for cut in pieces[1:]:
        level = level * one(*cut)
    return level


def gaussian(rng, shape, deviation, reach, shards=(), held_as=jnp.bfloat16):
    result = jax.random.normal(rng, shape, jnp.float32) * deviation
    if len(shards) > 0:
        result = levels(rng, shape, shards, -0.22, 0.18) * result
    return jnp.clip(result, min=-reach, max=reach).astype(held_as)


def setup_inputs(seed: int = 0) -> dict:
    splits = jax.random.split(jax.random.key(seed), 8)
    return {
        "queries": gaussian(splits[0], (N_TA, N_HA, N_WA, TILE, F), 1.0, 6.0, ((0, 2), (1, 4), (2, 4))),
        "current_kv": gaussian(splits[1], (N_TA, N_HA, N_WA, 2, TILE, F), 3.0, 18.0, ((0, 2), (1, 4), (2, 4))),
        "stale_kv": gaussian(splits[2], (N_TA, N_HA, N_WA, 2, TILE, F), 3.0, 18.0, ((0, 2), (1, 4), (2, 4))),
        "text_kv": gaussian(splits[3], (2, TEXT, F), 3.0, 18.0, ((1, 4),)),
        "q_gain": jnp.clip(jnp.exp(jax.random.uniform(splits[4], (HD,), jnp.float32, math.log(0.8), math.log(1.8))), 0.8, 1.8),
        "k_gain": jnp.clip(jnp.exp(jax.random.uniform(splits[5], (HD,), jnp.float32, math.log(0.8), math.log(1.8))), 0.8, 1.8),
        "pattern": touch_ends((jax.random.randint(splits[6], (N_TA, N_HA, N_WA, OFFSETS), 0, 2) < 1).astype(jnp.int32), jax.random.fold_in(splits[6], 1), 0, 1),
    }


offset_t = np.array([o // 9 - 1 for o in range(27)])
offset_h = np.array([o // 3 % 3 - 1 for o in range(27)])
offset_w = np.array([o % 3 - 1 for o in range(27)])

def qk_normed(values, gain):
    shaped = values.astype(jnp.float32).reshape(values.shape[:-1] + (HEADS, HD))
    square = lax.optimization_barrier(jnp.mean(shaped * shaped, axis=-1, keepdims=True))
    return (shaped * lax.rsqrt(square + 1e-06) * gain).reshape(values.shape).astype(jnp.bfloat16)

def reference(queries, current_kv, stale_kv, text_kv, q_gain, k_gain, pattern):
    scale = HD ** (-0.5)
    query_all = qk_normed(queries, q_gain)
    local_keys = qk_normed(current_kv[:, :, :, 0], k_gain)
    local_vals = current_kv[:, :, :, 1]
    stale_keys = qk_normed(stale_kv[:, :, :, 0], k_gain)
    stale_vals = stale_kv[:, :, :, 1]
    widths = ((1, 1), (1, 1), (1, 1), (0, 0), (0, 0))
    padded_keys = jnp.pad(stale_keys, widths)
    padded_vals = jnp.pad(stale_vals, widths)
    text_keys = qk_normed(text_kv[0], k_gain)
    text_vals = text_kv[1]
    step_t = jnp.asarray(offset_t, jnp.int32)
    step_h = jnp.asarray(offset_h, jnp.int32)
    step_w = jnp.asarray(offset_w, jnp.int32)
    centre = jnp.arange(27) == 13
    zero = jnp.zeros((), jnp.int32)

    def one_tile(index):
        index = index.astype(jnp.int32)
        tpos = index // (N_HA * N_WA)
        hpos = index // N_WA % N_HA
        wpos = index % N_WA
        start = (tpos, hpos, wpos, zero, zero)
        near_keys = lax.dynamic_slice(padded_keys, start, (3, 3, 3, TILE, F))
        near_vals = lax.dynamic_slice(padded_vals, start, (3, 3, 3, TILE, F))
        near_keys = near_keys.at[1, 1, 1].set(local_keys[tpos, hpos, wpos])
        near_vals = near_vals.at[1, 1, 1].set(local_vals[tpos, hpos, wpos])
        place_t = tpos + step_t
        place_h = hpos + step_h
        place_w = wpos + step_w
        inside = (place_t >= 0) & (place_t < N_TA) & (place_h >= 0) & (place_h < N_HA) & (place_w >= 0) & (place_w < N_WA)
        chosen = inside & ((pattern[tpos, hpos, wpos] == 1) | centre)
        key_mask = jnp.concatenate([jnp.repeat(chosen, TILE), jnp.ones((TEXT,), bool)])
        keys = jnp.concatenate([near_keys.reshape(27 * TILE, F), text_keys], axis=0)
        vals = jnp.concatenate([near_vals.reshape(27 * TILE, F), text_vals], axis=0)
        query_rows = query_all[tpos, hpos, wpos].astype(jnp.float32).reshape(TILE, HEADS, HD)
        keys = keys.astype(jnp.float32).reshape(-1, HEADS, HD)
        vals = vals.astype(jnp.float32).reshape(-1, HEADS, HD)
        scores = jnp.einsum('qhd,khd->hqk', query_rows, keys) * scale
        expo = jnp.where(key_mask[None, None, :], jnp.exp(scores), 0.0)
        weight = lax.optimization_barrier(jnp.sum(expo, axis=-1))
        rounded = expo.astype(jnp.bfloat16).astype(jnp.float32)
        total = jnp.einsum('hqk,khd->qhd', rounded, vals)
        return (total / weight.T[:, :, None]).reshape(TILE, F).astype(jnp.bfloat16)
    tiles = lax.map(one_tile, jnp.arange(N_TA * N_HA * N_WA, dtype=jnp.int32))
    return tiles.reshape(N_TA, N_HA, N_WA, TILE, F)
```

```python
import jax
import jax.numpy as jnp
from jax import lax
from jax.experimental import pallas as pl
from jax.experimental.pallas import tpu as pltpu
from jax.sharding import PartitionSpec as P

EPS = 1e-06
LANES = 128
IN_VMEM = pl.BlockSpec(memory_space=pltpu.VMEM)


def parities(count):
    return [parity for parity in (0, 1) if count - parity >= 2]


def step_of(place, parity):
    return jnp.where(place % 2 == parity, 1, -1)


def matching(axis_size, ta_size, parity):
    pairs = []
    for t in range(ta_size):
        for a in range(axis_size):
            b = a + 1 if a % 2 == parity else a - 1
            if 0 <= b < axis_size:
                pairs.append((t * axis_size + a, t * axis_size + b))
            elif t ^ 1 < ta_size:
                pairs.append((t * axis_size + a, (t ^ 1) * axis_size + a))
    return pairs


def swap_along(values, axis, parity):
    pairs = matching(lax.axis_size(axis), lax.axis_size("ta"), parity)
    return lax.ppermute(values, ("ta", axis), pairs)


def swap_ta(values, parity):
    count = lax.axis_size("ta")
    pairs = []
    for t in range(count):
        u = t + 1 if t % 2 == parity else t - 1
        if 0 <= u < count:
            pairs.append((t, u))
    return lax.ppermute(values, "ta", pairs)


def resident(values):
    return pltpu.with_memory_space_constraint(values, pltpu.VMEM)


def call(body, out_shape, *operands, flops=0, exps=0):
    outs = [pltpu.VMEM(s.shape, s.dtype) for s in out_shape]
    moved = sum(x.size * x.dtype.itemsize for x in operands)
    return pl.pallas_call(
        body,
        out_shape=outs,
        in_specs=[IN_VMEM] * len(operands),
        out_specs=[IN_VMEM] * len(outs),
        cost_estimate=pl.CostEstimate(flops=flops, bytes_accessed=moved, transcendentals=exps),
    )(*[resident(x) for x in operands])


def head_normed(values, gain, heads):
    hd = gain.shape[-1]
    parts = []
    for head in range(heads):
        part = values[:, head * hd : (head + 1) * hd]
        square = jnp.mean(part * part, axis=-1, keepdims=True)
        parts.append(part * lax.rsqrt(square + EPS) * gain)
    return jnp.concatenate(parts, axis=1)


def scores_of(q, k):
    return lax.dot_general(q, k, (((1,), (1,)), ((), ())), preferred_element_type=jnp.float32)


def prepare_queries(queries, q_gain, mask_rows):
    tile, width = queries.shape
    heads = width // q_gain.shape[-1]

    def body(q_ref, gain_ref, mask_ref, out_ref):
        normed = head_normed(q_ref[...].astype(jnp.float32), gain_ref[...], heads)
        masks = mask_ref[...]
        pad = jnp.zeros((masks.shape[0], width - masks.shape[1]), jnp.float32)
        rows = jnp.concatenate([masks, pad], axis=1)
        out_ref[...] = jnp.concatenate([normed, rows], axis=0).astype(jnp.bfloat16)

    shape = jax.ShapeDtypeStruct((tile + mask_rows.shape[0], width), jnp.bfloat16)
    return call(body, [shape], queries, q_gain, mask_rows)[0]


def attend_for_partners(slots, sent, k_gain, tile):
    rows, width = sent[0].shape if sent else (tile + 8, slots[0].shape[1])
    hd = k_gain.shape[-1]
    heads = width // hd
    count = len(slots)
    keys = count * tile
    scale = hd ** (-0.5)

    def body(*refs):
        slot_refs = refs[:count]
        sent_refs = refs[count : count + len(sent)]
        gain_ref = refs[count + len(sent)]
        outs = refs[count + len(sent) + 1 :]
        keys_ref, vals_ref = outs[0], outs[1]
        back_refs = outs[2:]
        gain = gain_ref[...]
        both = [r[...].astype(jnp.float32) for r in slot_refs]
        keys_ref[...] = jnp.concatenate(
            [head_normed(b[:tile], gain, heads) for b in both], axis=0
        ).astype(jnp.bfloat16)
        vals_ref[...] = jnp.concatenate([b[tile:] for b in both], axis=0).astype(jnp.bfloat16)
        if not sent:
            return
        q_all = jnp.concatenate([r[...] for r in sent_refs], axis=0)
        masks = []
        for index, r in enumerate(sent_refs):
            row = r[...].astype(jnp.float32)[tile + index : tile + index + 1, :keys]
            masks.append(jnp.broadcast_to(row, (rows, keys)))
        mask = jnp.concatenate(masks, axis=0)
        lane = lax.broadcasted_iota(jnp.int32, (len(sent) * rows, LANES), 1)
        sums = jnp.zeros((len(sent) * rows, LANES), jnp.float32)
        for head in range(heads):
            cols = slice(head * hd, (head + 1) * hd)
            expo = jnp.exp(scores_of(q_all[:, cols], keys_ref[:, cols]) * scale) * mask
            total = jnp.dot(
                expo.astype(jnp.bfloat16), vals_ref[:, cols], preferred_element_type=jnp.float32
            )
            weight = jnp.sum(expo, axis=1, keepdims=True)
            high = weight.astype(jnp.bfloat16).astype(jnp.float32)
            sums = jnp.where(lane == head, high, sums)
            sums = jnp.where(lane == head + LANES // 2, weight - high, sums)
            for index, back in enumerate(back_refs):
                back[:, cols] = total[index * rows : index * rows + tile].astype(jnp.bfloat16)
        for index, back in enumerate(back_refs):
            back[:, width:] = sums[index * rows : index * rows + tile].astype(jnp.bfloat16)

    shapes = [jax.ShapeDtypeStruct((keys, width), jnp.bfloat16)] * 2
    shapes += [jax.ShapeDtypeStruct((tile, width + LANES), jnp.bfloat16)] * len(sent)
    outs = call(
        body,
        shapes,
        *slots,
        *sent,
        k_gain,
        flops=4 * len(sent) * rows * keys * width,
        exps=len(sent) * rows * keys * heads,
    )
    return outs[0], outs[1], outs[2:]


def attend_own(own, keys, vals, current, text_keys, text_vals, k_gain, tile, mask_row):
    rows, width = own.shape
    hd = k_gain.shape[-1]
    heads = width // hd
    count = keys.shape[0]
    scale = hd ** (-0.5)

    def body(q_ref, keys_ref, vals_ref, current_ref, text_k_ref, text_v_ref, gain_ref, total_ref, sum_ref):
        gain = gain_ref[...]
        here = current_ref[...].astype(jnp.float32)
        sure_keys = jnp.concatenate(
            [
                head_normed(here[:tile], gain, heads),
                head_normed(text_k_ref[...].astype(jnp.float32), gain, heads),
            ],
            axis=0,
        ).astype(jnp.bfloat16)
        sure_vals = jnp.concatenate(
            [here[tile:], text_v_ref[...].astype(jnp.float32)], axis=0
        ).astype(jnp.bfloat16)
        q = q_ref[...]
        mask = q.astype(jnp.float32)[tile + mask_row : tile + mask_row + 1, :count]
        lane = lax.broadcasted_iota(jnp.int32, (rows, LANES), 1)
        sums = jnp.ones((rows, LANES), jnp.float32)
        for head in range(heads):
            cols = slice(head * hd, (head + 1) * hd)
            near = jnp.exp(scores_of(q[:, cols], keys_ref[:, cols]) * scale) * mask
            sure = jnp.exp(scores_of(q[:, cols], sure_keys[:, cols]) * scale)
            total = jnp.dot(
                near.astype(jnp.bfloat16), vals_ref[:, cols], preferred_element_type=jnp.float32
            ) + jnp.dot(
                sure.astype(jnp.bfloat16), sure_vals[:, cols], preferred_element_type=jnp.float32
            )
            weight = jnp.sum(near, axis=1, keepdims=True) + jnp.sum(sure, axis=1, keepdims=True)
            sums = jnp.where(lane == head, weight, sums)
            total_ref[:, cols] = total[:tile]
        sum_ref[...] = sums[:tile]

    shapes = [
        jax.ShapeDtypeStruct((tile, width), jnp.float32),
        jax.ShapeDtypeStruct((tile, LANES), jnp.float32),
    ]
    all_keys = count + tile + text_keys.shape[0]
    return call(
        body,
        shapes,
        own,
        keys,
        vals,
        current,
        text_keys,
        text_vals,
        k_gain,
        flops=4 * rows * all_keys * width,
        exps=rows * all_keys * heads,
    )


def combine(total, weight, backs, hd):
    tile, width = total.shape
    heads = width // hd

    def body(total_ref, sum_ref, *refs):
        back_refs, out_ref = refs[:-1], refs[-1]
        sums = sum_ref[...]
        for r in back_refs:
            part = r[:, width:].astype(jnp.float32)
            sums = sums + part + pltpu.roll(part, LANES // 2, 1)
        inverse = 1.0 / sums
        for head in range(heads):
            cols = slice(head * hd, (head + 1) * hd)
            whole = total_ref[:, cols]
            for r in back_refs:
                whole = whole + r[:, cols].astype(jnp.float32)
            out_ref[:, cols] = (whole * inverse[:, head : head + 1]).astype(jnp.bfloat16)

    operands = [total, weight, *backs]
    return pl.pallas_call(
        body,
        out_shape=jax.ShapeDtypeStruct((tile, width), jnp.bfloat16),
        in_specs=[IN_VMEM] * len(operands),
        out_specs=IN_VMEM,
    )(*[resident(x) for x in operands])


def gather_text(text_kv):
    count = lax.axis_size("wa")
    if count & (count - 1):
        return lax.all_gather(text_kv, "wa", axis=1, tiled=True)
    span = 1
    while span < count:
        other = lax.ppermute(text_kv, "wa", [(i, i ^ span) for i in range(count)])
        text_kv = jnp.concatenate([text_kv, other], axis=1)
        span *= 2
    return text_kv


def mask_rows_of(pattern, tile, row_count):
    place = {a: lax.axis_index(a) for a in ("ta", "ha", "wa")}
    size = {a: lax.axis_size(a) for a in ("ta", "ha", "wa")}
    steps = {a: [step_of(place[a], p) for p in parities(size[a])] for a in size}
    steps_t = [0] + steps["ta"]
    steps_w = [0] + steps["wa"]
    steps_h = steps["ha"] + [0]
    count = len(steps_t) * len(steps_w)
    lanes = -(-count * tile // LANES) * LANES
    slot = lax.broadcasted_iota(jnp.int32, (row_count, lanes), 1) // tile
    row = lax.broadcasted_iota(jnp.int32, (row_count, lanes), 0)

    def pick(index, options):
        chosen = jnp.full((row_count, lanes), 9, jnp.int32)
        for i, option in enumerate(options):
            chosen = jnp.where(index == i, option, chosen)
        return chosen

    dt = pick(slot // len(steps_w), steps_t)
    dw = pick(slot % len(steps_w), steps_w)
    dh = pick(row, steps_h)
    inside = jnp.ones((row_count, lanes), bool)
    for axis, d in (("ta", dt), ("ha", dh), ("wa", dw)):
        inside = inside & (d < 9) & (place[axis] + d >= 0) & (place[axis] + d < size[axis])
    offset = (dt + 1) * 9 + (dh + 1) * 3 + dw + 1
    used = inside & (offset != 13)
    hits = jnp.zeros((row_count, lanes), bool)
    for o in range(27):
        hits = hits | ((offset == o) & (pattern[o] == 1))
    return jnp.where(used & hits, 1.0, 0.0).astype(jnp.float32)


def shards(queries, current_kv, stale_kv, text_kv, q_gain, k_gain, pattern):
    tile, width = queries.shape[3:]
    hd = q_gain.shape[0]
    stale = stale_kv.reshape(2 * tile, width)
    current = current_kv.reshape(2 * tile, width)
    k_gain = k_gain.reshape(1, hd)
    h_parities = parities(lax.axis_size("ha"))

    line = [stale] + [swap_along(stale, "wa", p) for p in parities(lax.axis_size("wa"))]
    mask_rows = mask_rows_of(pattern.reshape(27), tile, 8)
    own = prepare_queries(queries.reshape(tile, width), q_gain.reshape(1, hd), mask_rows)
    sent = [swap_along(own, "ha", p) for p in h_parities]
    text = gather_text(text_kv)
    slots = list(line)
    for p in parities(lax.axis_size("ta")):
        slots += [swap_ta(x, p) for x in line]
    keys, vals, answers = attend_for_partners(slots, sent, k_gain, tile)
    backs = [swap_along(x, "ha", p) for x, p in zip(answers, h_parities, strict=True)]
    total, weight = attend_own(
        own, keys, vals, current, text[0], text[1], k_gain, tile, len(h_parities)
    )
    result = combine(total, weight, backs, hd)
    return result.reshape(1, 1, 1, tile, width)


def solution(mesh):
    return jax.shard_map(
        shards,
        mesh=mesh,
        in_specs=(
            P("ta", "ha", "wa", None, None),
            P("ta", "ha", "wa", None, None, None),
            P("ta", "ha", "wa", None, None, None),
            P(None, "wa", None),
            P(),
            P(),
            P("ta", "ha", "wa", None),
        ),
        out_specs=P("ta", "ha", "wa", None, None),
        check_vma=False,
    )
```

```python
import jax
import jax.numpy as jnp
from jax import lax
from jax.experimental import pallas as pl
from jax.experimental.pallas import tpu as pltpu
from jax.sharding import PartitionSpec as P

EPS = 1e-06
LANES = 128
IN_VMEM = pl.BlockSpec(memory_space=pltpu.VMEM)
IN_SMEM = pl.BlockSpec(memory_space=pltpu.SMEM)


def parities(count):
    return [parity for parity in (0, 1) if count - parity >= 2]


def matching(axis_size, ta_size, parity):
    pairs = []
    for t in range(ta_size):
        for a in range(axis_size):
            b = a + 1 if a % 2 == parity else a - 1
            if 0 <= b < axis_size:
                pairs.append((t * axis_size + a, t * axis_size + b))
            elif t ^ 1 < ta_size:
                pairs.append((t * axis_size + a, (t ^ 1) * axis_size + a))
    return pairs


def swap_along(values, axis, parity):
    pairs = matching(lax.axis_size(axis), lax.axis_size("ta"), parity)
    return lax.ppermute(values, ("ta", axis), pairs)


def swap_ta(values, parity):
    count = lax.axis_size("ta")
    pairs = []
    for t in range(count):
        u = t + 1 if t % 2 == parity else t - 1
        if 0 <= u < count:
            pairs.append((t, u))
    return lax.ppermute(values, "ta", pairs)


def resident(values):
    return pltpu.with_memory_space_constraint(values, pltpu.VMEM)


def call(body, out_shape, *operands, flops=0, exps=0):
    outs = [pltpu.VMEM(s.shape, s.dtype) for s in out_shape]
    moved = sum(x.size * x.dtype.itemsize for x in operands)
    return pl.pallas_call(
        body,
        out_shape=outs,
        in_specs=[IN_VMEM] * len(operands),
        out_specs=[IN_VMEM] * len(outs),
        cost_estimate=pl.CostEstimate(flops=flops, bytes_accessed=moved, transcendentals=exps),
    )(*[resident(x) for x in operands])


def head_normed(values, gain, heads):
    hd = gain.shape[-1]
    parts = []
    for head in range(heads):
        part = values[:, head * hd : (head + 1) * hd]
        square = jnp.mean(part * part, axis=-1, keepdims=True)
        parts.append(part * lax.rsqrt(square + EPS) * gain)
    return jnp.concatenate(parts, axis=1)


def split(values, heads):
    hd = values.shape[1] // heads
    return [values[:, head * hd : (head + 1) * hd] for head in range(heads)]


def attention(queries, groups, heads):
    scale = (queries.shape[1] // heads) ** (-0.5)
    queries = split(queries, heads)
    totals, weights = [0.0] * heads, [0.0] * heads
    for keys, vals, mask in groups:
        scores = [
            lax.dot_general(q, k, (((1,), (1,)), ((), ())), preferred_element_type=jnp.float32)
            for q, k in zip(queries, split(keys, heads), strict=True)
        ]
        expos = [jnp.exp(x * scale) for x in scores]
        if mask is not None:
            expos = [x * mask for x in expos]
        sums = [
            jnp.dot(x.astype(jnp.bfloat16), v, preferred_element_type=jnp.float32)
            for x, v in zip(expos, split(vals, heads), strict=True)
        ]
        totals = [x + y for x, y in zip(totals, sums, strict=True)]
        weights = [x + jnp.sum(y, axis=1, keepdims=True) for x, y in zip(weights, expos, strict=True)]
    return totals, weights


def in_lanes(columns):
    lane = lax.broadcasted_iota(jnp.int32, (columns[0].shape[0], LANES), 1)
    rows = jnp.zeros(lane.shape, jnp.float32)
    for h, column in enumerate(columns):
        rows = jnp.where(lane == h, column, rows)
    return rows


def normed_tiles(both, gain, heads, tile):
    both = [b.astype(jnp.float32) for b in both]
    keys = jnp.concatenate([head_normed(b[:tile], gain, heads) for b in both], axis=0)
    vals = jnp.concatenate([b[tile:] for b in both], axis=0)
    return keys.astype(jnp.bfloat16), vals.astype(jnp.bfloat16)


def slot_flags(pattern_ref, axes, sizes, rows):
    place = [lax.axis_index(a) for a in axes]
    steps_h, steps_w = (
        [jnp.where(place[i] % 2 == parity, 1, -1) for parity in parities(sizes[i])] for i in (1, 2)
    )
    lane = lax.broadcasted_iota(jnp.int32, (rows, LANES), 1)
    row = lax.broadcasted_iota(jnp.int32, (rows, LANES), 0)
    flags = jnp.zeros((rows, LANES), jnp.float32)
    for r, dh in enumerate([*steps_h, 0]):
        slot = 0
        for t in range(sizes[0]):
            dt = t - place[0]
            for dw in [0, *steps_w]:
                inside = (dt >= -1) & (dt <= 1)
                for i, d in ((1, dh), (2, dw)):
                    inside = inside & (place[i] + d >= 0) & (place[i] + d < sizes[i])
                offset = (jnp.clip(dt, -1, 1) + 1) * 9 + (dh + 1) * 3 + dw + 1
                used = jnp.where(inside & (pattern_ref[offset] == 1) & (offset != 13), 1.0, 0.0)
                flags = jnp.where((row == r) & (lane == slot), used, flags)
                slot += 1
    return flags


def key_masks(flags, places, line, tile):
    masks = []
    for t in range(places):
        lane = lax.broadcasted_iota(jnp.int32, (1, line * tile), 1) // tile
        mask = jnp.zeros(lane.shape, jnp.float32)
        for i in range(line):
            slot = t * line + i
            mask = jnp.where(lane == i, flags[:, slot : slot + 1], mask)
        masks.append(mask)
    return masks


def prepare(queries, q_gain, pattern, axes, sizes):
    tile, width = queries.shape
    heads = width // q_gain.shape[-1]

    def body(q_ref, gain_ref, pattern_ref, out_ref):
        normed = head_normed(q_ref[...].astype(jnp.float32), gain_ref[...], heads)
        flags = slot_flags(pattern_ref, axes, sizes, tile)
        out_ref[...] = jnp.concatenate([normed, flags], axis=1).astype(jnp.bfloat16)

    return pl.pallas_call(
        body,
        out_shape=pltpu.VMEM((tile, width + LANES), jnp.bfloat16),
        in_specs=[IN_VMEM, IN_VMEM, IN_SMEM],
        out_specs=IN_VMEM,
    )(queries, q_gain, pattern)


def norm_line(slots, text, k_gain, tile):
    width = slots[0].shape[1]
    heads = width // k_gain.shape[-1]

    def body(*refs):
        slot_refs, (text_ref, gain_ref, line_ref, text_out_ref) = refs[:-4], refs[-4:]
        gain = gain_ref[...]
        keys, vals = normed_tiles([r[...] for r in slot_refs], gain, heads, tile)
        text_keys = head_normed(text_ref[0].astype(jnp.float32), gain, heads)
        line_ref[:, :width] = keys
        line_ref[:, width:] = vals
        text_out_ref[0] = text_keys.astype(jnp.bfloat16)
        text_out_ref[1] = text_ref[1]

    shapes = [
        jax.ShapeDtypeStruct((len(slots) * tile, 2 * width), jnp.bfloat16),
        jax.ShapeDtypeStruct(text.shape, text.dtype),
    ]
    return call(body, shapes, *slots, text, k_gain)


def attend_partners(around, sent, tile, hd):
    places, rows, width = around.shape
    width //= 2
    line = rows // tile
    heads = width // hd

    def body(around_ref, *refs):
        sent_refs, back_refs = refs[: len(sent)], refs[len(sent) :]
        blocks = [r[...].astype(jnp.float32) for r in sent_refs]
        masks = [
            key_masks(block[i : i + 1, width:], places, line, tile) for i, block in enumerate(blocks)
        ]
        groups = []
        for t in range(places):
            mask = [jnp.broadcast_to(m[t], (tile, rows)) for m in masks]
            groups.append(
                (around_ref[t, :, :width], around_ref[t, :, width:], jnp.concatenate(mask, axis=0))
            )
        queries = jnp.concatenate([b[:, :width] for b in blocks], axis=0).astype(jnp.bfloat16)
        totals, weights = attention(queries, groups, heads)
        sums = in_lanes(weights)
        high = sums.astype(jnp.bfloat16).astype(jnp.float32)
        packed = high + pltpu.roll(sums - high, LANES // 2, 1)
        whole = jnp.concatenate([*totals, packed], axis=1)
        for i, back in enumerate(back_refs):
            back[...] = whole[i * tile : (i + 1) * tile].astype(jnp.bfloat16)

    shapes = [jax.ShapeDtypeStruct((tile, width + LANES), jnp.bfloat16)] * len(sent)
    return call(body, shapes, around, *sent)


def attend_own(own, around, current, text, k_gain, tile, reader):
    places, rows, width = around.shape
    width //= 2
    line = rows // tile
    heads = width // k_gain.shape[-1]

    def body(own_ref, around_ref, current_ref, gain_ref, *refs):
        text_refs, (total_ref, sum_ref) = refs[:-2], refs[-2:]
        here = current_ref[...].astype(jnp.float32)
        sure_keys = [head_normed(here[:tile], gain_ref[...], heads)]
        sure_vals = [here[tile:]]
        for r in text_refs:
            sure_keys.append(r[0].astype(jnp.float32))
            sure_vals.append(r[1].astype(jnp.float32))
        sure_keys, sure_vals = (
            jnp.concatenate(x, axis=0).astype(jnp.bfloat16) for x in (sure_keys, sure_vals)
        )
        flags = own_ref[:, width:].astype(jnp.float32)[reader : reader + 1]
        masks = key_masks(flags, places, line, tile)
        groups = [(sure_keys, sure_vals, None)]
        for t in range(places):
            groups.append((around_ref[t, :, :width], around_ref[t, :, width:], masks[t]))
        totals, weights = attention(own_ref[:, :width], groups, heads)
        total_ref[...] = jnp.concatenate(totals, axis=1)
        sum_ref[...] = in_lanes(weights)

    shapes = [
        jax.ShapeDtypeStruct((tile, width), jnp.float32),
        jax.ShapeDtypeStruct((tile, LANES), jnp.float32),
    ]
    return call(body, shapes, own, around, current, k_gain, *text)


def combine(total, weight, backs, hd):
    tile, width = total.shape
    heads = width // hd

    def body(total_ref, sum_ref, *refs):
        back_refs, out_ref = refs[:-1], refs[-1]
        parts = [r[...].astype(jnp.float32) for r in back_refs]
        whole, sums = total_ref[...], sum_ref[...]
        for part in parts:
            tail = part[:, width:]
            whole = whole + part[:, :width]
            sums = sums + tail + pltpu.roll(tail, LANES // 2, 1)
        inverse = 1.0 / jnp.where(lax.broadcasted_iota(jnp.int32, sums.shape, 1) < heads, sums, 1.0)
        scaled = [x * inverse[:, h : h + 1] for h, x in enumerate(split(whole, heads))]
        out_ref[...] = jnp.concatenate(scaled, axis=1).astype(jnp.bfloat16)

    operands = [total, weight, *backs]
    return pl.pallas_call(
        body,
        out_shape=jax.ShapeDtypeStruct((tile, width), jnp.bfloat16),
        in_specs=[IN_VMEM] * len(operands),
        out_specs=IN_VMEM,
    )(*[resident(x) for x in operands])


def gather_text(text):
    count, cores = lax.axis_size("wa"), lax.axis_size("ta")
    if count & (count - 1):
        return [lax.all_gather(text, "wa", axis=1, tiled=True)]
    near = lax.ppermute(text, "wa", [(i, i ^ 1) for i in range(count)]) if count > 1 else None
    if count == 4 and cores % 2 == 0:
        pairs = [(t * 4 + i, t * 4 + (i ^ (2 + t % 2))) for t in range(cores) for i in range(4)]
        far = lax.ppermute(text, ("ta", "wa"), pairs)
        return [text, near, far, swap_ta(far, 0)]
    if count > 1:
        text = jnp.concatenate([text, near], axis=1)
    span = 2
    while span < count:
        other = lax.ppermute(text, "wa", [(i, i ^ span) for i in range(count)])
        text = jnp.concatenate([text, other], axis=1)
        span *= 2
    return [text]


def shards(queries, current_kv, stale_kv, text_kv, q_gain, k_gain, pattern):
    tile, width = queries.shape[3:]
    hd = q_gain.shape[0]
    stale = stale_kv.reshape(2 * tile, width)
    current = current_kv.reshape(2 * tile, width)
    k_gain = k_gain.reshape(1, hd)
    axes = ("ta", "ha", "wa")
    sizes = [lax.axis_size(a) for a in axes]
    parities_h, parities_w = parities(sizes[1]), parities(sizes[2])

    line = [stale] + [swap_along(stale, "wa", p) for p in parities_w]
    own = prepare(
        queries.reshape(tile, width), q_gain.reshape(1, hd), pattern.reshape(27), axes, sizes
    )
    sent = [swap_along(own, "ha", p) for p in parities_h]
    line_kv, text = norm_line(line, text_kv, k_gain, tile)
    around = lax.all_gather(line_kv, "ta")
    text = gather_text(text)
    answers = attend_partners(around, sent, tile, hd)
    backs = [swap_along(x, "ha", p) for x, p in zip(answers, parities_h, strict=True)]
    total, weight = attend_own(own, around, current, text, k_gain, tile, len(parities_h))
    result = combine(total, weight, backs, hd)
    return result.reshape(1, 1, 1, tile, width)


def solution(mesh):
    return jax.shard_map(
        shards,
        mesh=mesh,
        in_specs=(
            P("ta", "ha", "wa", None, None),
            P("ta", "ha", "wa", None, None, None),
            P("ta", "ha", "wa", None, None, None),
            P(None, "wa", None),
            P(),
            P(),
            P("ta", "ha", "wa", None),
        ),
        out_specs=P("ta", "ha", "wa", None, None),
        check_vma=False,
    )
```

```python
import jax
import jax.numpy as jnp
from jax import lax
from jax.experimental import pallas as pl
from jax.experimental.pallas import tpu as pltpu
from jax.sharding import PartitionSpec as P

EPS = 1e-06
LANES = 128
IN_VMEM = pl.BlockSpec(memory_space=pltpu.VMEM)
IN_SMEM = pl.BlockSpec(memory_space=pltpu.SMEM)


def parities(count):
    return [parity for parity in (0, 1) if count - parity >= 2]


def matching(axis_size, ta_size, parity):
    pairs = []
    for t in range(ta_size):
        for a in range(axis_size):
            b = a + 1 if a % 2 == parity else a - 1
            if 0 <= b < axis_size:
                pairs.append((t * axis_size + a, t * axis_size + b))
            elif t ^ 1 < ta_size:
                pairs.append((t * axis_size + a, (t ^ 1) * axis_size + a))
    return pairs


def swap_along(values, axis, parity):
    pairs = matching(lax.axis_size(axis), lax.axis_size("ta"), parity)
    return lax.ppermute(values, ("ta", axis), pairs)


def swap_ta(values, parity):
    count = lax.axis_size("ta")
    pairs = []
    for t in range(count):
        u = t + 1 if t % 2 == parity else t - 1
        if 0 <= u < count:
            pairs.append((t, u))
    return lax.ppermute(values, "ta", pairs)


def resident(values):
    return pltpu.with_memory_space_constraint(values, pltpu.VMEM)


def call(body, out_shape, *operands, flops=0):
    outs = [pltpu.VMEM(s.shape, s.dtype) for s in out_shape]
    moved = sum(x.size * x.dtype.itemsize for x in operands)
    return pl.pallas_call(
        body,
        out_shape=outs,
        in_specs=[IN_VMEM] * len(operands),
        out_specs=[IN_VMEM] * len(outs),
        cost_estimate=pl.CostEstimate(flops=flops, bytes_accessed=moved, transcendentals=0),
    )(*[resident(x) for x in operands])


def head_normed(values, gain, heads):
    hd = gain.shape[-1]
    parts = []
    for head in range(heads):
        part = values[:, head * hd : (head + 1) * hd]
        square = jnp.mean(part * part, axis=-1, keepdims=True)
        parts.append(part * lax.rsqrt(square + EPS) * gain)
    return jnp.concatenate(parts, axis=1)


def split(values, heads):
    hd = values.shape[1] // heads
    return [values[:, head * hd : (head + 1) * hd] for head in range(heads)]


def attention(queries, groups, heads):
    scale = (queries.shape[1] // heads) ** (-0.5)
    queries = split(queries, heads)
    totals, weights = [0.0] * heads, [0.0] * heads
    for keys, vals, mask in groups:
        scores = [
            lax.dot_general(q, k, (((1,), (1,)), ((), ())), preferred_element_type=jnp.float32)
            for q, k in zip(queries, split(keys, heads), strict=True)
        ]
        expos = [jnp.exp(x * scale) for x in scores]
        if mask is not None:
            expos = [x * mask for x in expos]
        sums = [
            jnp.dot(x.astype(jnp.bfloat16), v, preferred_element_type=jnp.float32)
            for x, v in zip(expos, split(vals, heads), strict=True)
        ]
        totals = [x + y for x, y in zip(totals, sums, strict=True)]
        weights = [x + jnp.sum(y, axis=1, keepdims=True) for x, y in zip(weights, expos, strict=True)]
    return totals, weights


def in_lanes(columns):
    lane = lax.broadcasted_iota(jnp.int32, (columns[0].shape[0], LANES), 1)
    rows = jnp.zeros(lane.shape, jnp.float32)
    for h, column in enumerate(columns):
        rows = jnp.where(lane == h, column, rows)
    return rows


def normed_tiles(both, gain, heads, tile):
    both = [b.astype(jnp.float32) for b in both]
    keys = jnp.concatenate([head_normed(b[:tile], gain, heads) for b in both], axis=0)
    vals = jnp.concatenate([b[tile:] for b in both], axis=0)
    return keys.astype(jnp.bfloat16), vals.astype(jnp.bfloat16)


def slot_flags(pattern_ref, axes, sizes, rows):
    place = [lax.axis_index(a) for a in axes]
    steps_h, steps_w = (
        [jnp.where(place[i] % 2 == parity, 1, -1) for parity in parities(sizes[i])] for i in (1, 2)
    )
    lane = lax.broadcasted_iota(jnp.int32, (rows, LANES), 1)
    row = lax.broadcasted_iota(jnp.int32, (rows, LANES), 0)
    flags = jnp.zeros((rows, LANES), jnp.float32)
    for r, dh in enumerate([*steps_h, 0]):
        slot = 0
        for t in range(sizes[0]):
            dt = t - place[0]
            for dw in [*steps_w[1:], 0, *steps_w[:1]]:
                inside = (dt >= -1) & (dt <= 1)
                for i, d in ((1, dh), (2, dw)):
                    inside = inside & (place[i] + d >= 0) & (place[i] + d < sizes[i])
                offset = (jnp.clip(dt, -1, 1) + 1) * 9 + (dh + 1) * 3 + dw + 1
                used = jnp.where(inside & (pattern_ref[offset] == 1) & (offset != 13), 1.0, 0.0)
                flags = jnp.where((row == r) & (lane == slot), used, flags)
                slot += 1
    return flags


def key_masks(flags, places, line, tile, rows):
    lane = lax.broadcasted_iota(jnp.int32, (1, rows), 1)
    masks = []
    for t in range(places):
        mask = jnp.zeros((1, rows), jnp.float32)
        for i in range(line):
            slot = t * line + i
            mask = jnp.where(lane // tile == i, flags[:, slot : slot + 1], mask)
        masks.append(mask)
    return masks


def prepare(queries, stale, text, q_gain, k_gain, pattern, axes, sizes):
    tile, width = queries.shape
    tokens = text.shape[1]
    heads = width // q_gain.shape[-1]
    folds = tile // tokens
    chunk = 2 * width // folds

    def body(q_ref, stale_ref, text_ref, q_gain_ref, k_gain_ref, pattern_ref, own_ref, pack_ref, text_out_ref):
        k_gain = k_gain_ref[...]
        normed = head_normed(q_ref[...].astype(jnp.float32), q_gain_ref[...], heads)
        flags = slot_flags(pattern_ref, axes, sizes, tile)
        own_ref[...] = jnp.concatenate([normed, flags], axis=1).astype(jnp.bfloat16)
        both = stale_ref[...].astype(jnp.float32)
        text_keys = head_normed(text_ref[0].astype(jnp.float32), k_gain, heads)
        words = jnp.concatenate([text_keys, text_ref[1].astype(jnp.float32)], axis=1)
        folded = [words[:, i * chunk : (i + 1) * chunk] for i in range(folds)]
        pack = [head_normed(both[:tile], k_gain, heads), both[tile:], jnp.concatenate(folded, axis=0)]
        pack_ref[...] = jnp.concatenate(pack, axis=1).astype(jnp.bfloat16)
        text_out_ref[...] = words.astype(jnp.bfloat16)

    shapes = [(tile, width + LANES), (tile, 2 * width + chunk), (tokens, 2 * width)]
    return pl.pallas_call(
        body,
        out_shape=[pltpu.VMEM(shape, jnp.bfloat16) for shape in shapes],
        in_specs=[IN_VMEM] * 5 + [IN_SMEM],
        out_specs=[IN_VMEM] * 3,
    )(queries, stale, text, q_gain, k_gain, pattern)


def norm_raw(both, k_gain, tile):
    width = both.shape[1]
    heads = width // k_gain.shape[-1]

    def body(both_ref, gain_ref, out_ref):
        both = both_ref[...].astype(jnp.float32)
        keys = head_normed(both[:tile], gain_ref[...], heads)
        out_ref[...] = jnp.concatenate([keys, both[tile:]], axis=1).astype(jnp.bfloat16)

    shape = jax.ShapeDtypeStruct((tile, 2 * width), jnp.bfloat16)
    return call(body, [shape], both, k_gain, flops=int(3e8))[0]


def join_line(packs, width):
    def body(*refs):
        parts = [r[:, : 2 * width].astype(jnp.float32) for r in refs[:-1]]
        refs[-1][...] = jnp.concatenate(parts, axis=0).astype(jnp.bfloat16)

    shape = jax.ShapeDtypeStruct((sum(x.shape[0] for x in packs), 2 * width), jnp.bfloat16)
    return call(body, [shape], *packs)[0]


def attend_partners(around, sent, far, tile, line, hd):
    places, rows, width = around.shape
    width //= 2
    heads = width // hd

    def body(around_ref, *refs):
        sent_refs, refs = refs[: len(sent)], refs[len(sent) :]
        far_refs, refs = refs[: len(far)], refs[len(far) :]
        back_refs, on_refs = refs[: len(sent)], refs[len(sent) :]
        for r, on in zip(far_refs, on_refs, strict=True):
            on[...] = r[...]
        blocks = [r[...].astype(jnp.float32) for r in sent_refs]
        masks = [
            key_masks(block[i : i + 1, width:], places, line, tile, rows)
            for i, block in enumerate(blocks)
        ]
        groups = []
        for t in range(places):
            mask = [jnp.broadcast_to(m[t], (tile, rows)) for m in masks]
            groups.append(
                (around_ref[t, :, :width], around_ref[t, :, width:], jnp.concatenate(mask, axis=0))
            )
        queries = jnp.concatenate([b[:, :width] for b in blocks], axis=0).astype(jnp.bfloat16)
        totals, weights = attention(queries, groups, heads)
        sums = in_lanes(weights)
        high = sums.astype(jnp.bfloat16).astype(jnp.float32)
        packed = high + pltpu.roll(sums - high, LANES // 2, 1)
        whole = jnp.concatenate([*totals, packed], axis=1)
        for i, back in enumerate(back_refs):
            back[...] = whole[i * tile : (i + 1) * tile].astype(jnp.bfloat16)

    shapes = [jax.ShapeDtypeStruct((tile, width + LANES), jnp.bfloat16)] * len(sent)
    shapes += [jax.ShapeDtypeStruct(x.shape, x.dtype) for x in far]
    outs = call(body, shapes, around, *sent, *far)
    return outs[: len(sent)], outs[len(sent) :]


def attend_own(own, around, current, words, near, k_gain, tile, line, reader):
    places, rows, width = around.shape
    width //= 2
    heads = width // k_gain.shape[-1]

    def body(own_ref, around_ref, current_ref, gain_ref, *refs):
        total_ref, sum_ref = refs[-2:]
        here = current_ref[...].astype(jnp.float32)
        keys = head_normed(here[:tile], gain_ref[...], heads)
        sure = [jnp.concatenate([keys, here[tile:]], axis=1)]
        sure += [r[...].astype(jnp.float32) for r in refs[: len(words)]]
        tokens = words[0].shape[0]
        for r in refs[len(words) : -2]:
            folded = r[:, 2 * width :].astype(jnp.float32)
            folds = [folded[i * tokens : (i + 1) * tokens] for i in range(tile // tokens)]
            sure.append(jnp.concatenate(folds, axis=1))
        sure = jnp.concatenate(sure, axis=0).astype(jnp.bfloat16)
        flags = own_ref[:, width:].astype(jnp.float32)[reader : reader + 1]
        masks = key_masks(flags, places, line, tile, rows)
        groups = [(sure[:, :width], sure[:, width:], None)]
        for t in range(places):
            groups.append((around_ref[t, :, :width], around_ref[t, :, width:], masks[t]))
        totals, weights = attention(own_ref[:, :width], groups, heads)
        total_ref[...] = jnp.concatenate(totals, axis=1)
        sum_ref[...] = in_lanes(weights)

    shapes = [
        jax.ShapeDtypeStruct((tile, width), jnp.float32),
        jax.ShapeDtypeStruct((tile, LANES), jnp.float32),
    ]
    return call(body, shapes, own, around, current, k_gain, *words, *near)


def combine(total, weight, backs, hd):
    tile, width = total.shape
    heads = width // hd

    def body(total_ref, sum_ref, *refs):
        back_refs, out_ref = refs[:-1], refs[-1]
        parts = [r[...].astype(jnp.float32) for r in back_refs]
        whole, sums = total_ref[...], sum_ref[...]
        for part in parts:
            tail = part[:, width:]
            whole = whole + part[:, :width]
            sums = sums + tail + pltpu.roll(tail, LANES // 2, 1)
        inverse = 1.0 / jnp.where(lax.broadcasted_iota(jnp.int32, sums.shape, 1) < heads, sums, 1.0)
        scaled = [x * inverse[:, h : h + 1] for h, x in enumerate(split(whole, heads))]
        out_ref[...] = jnp.concatenate(scaled, axis=1).astype(jnp.bfloat16)

    operands = [total, weight, *backs]
    return pl.pallas_call(
        body,
        out_shape=jax.ShapeDtypeStruct((tile, width), jnp.bfloat16),
        in_specs=[IN_VMEM] * len(operands),
        out_specs=IN_VMEM,
    )(*[resident(x) for x in operands])


def shards(queries, current_kv, stale_kv, text_kv, q_gain, k_gain, pattern):
    tile, width = queries.shape[3:]
    hd = q_gain.shape[0]
    stale = stale_kv.reshape(2 * tile, width)
    current = current_kv.reshape(2 * tile, width)
    k_gain = k_gain.reshape(1, hd)
    axes = ("ta", "ha", "wa")
    sizes = [lax.axis_size(a) for a in axes]
    parities_h, parities_w = parities(sizes[1]), parities(sizes[2])

    raw = [norm_raw(swap_along(stale, "wa", p), k_gain, tile) for p in parities_w[1:]]
    own, pack, words = prepare(
        queries.reshape(tile, width),
        stale,
        text_kv,
        q_gain.reshape(1, hd),
        k_gain,
        pattern.reshape(27),
        axes,
        sizes,
    )
    packs = [pack] + [swap_along(pack, "wa", p) for p in parities_w[:1]]
    sent = [swap_along(own, "ha", p) for p in parities_h]
    near, far = [], []
    if sizes[2] == 4 and sizes[0] % 2 == 0:
        pairs = [(t * 4 + i, t * 4 + (i ^ (2 + t % 2))) for t in range(sizes[0]) for i in range(4)]
        near, far = packs[1:], [lax.ppermute(words, ("ta", "wa"), pairs)]
        words = [words]
    else:
        words = [lax.all_gather(words, "wa", axis=0, tiled=True)]
    packs = raw + packs
    line = len(packs)
    around = lax.all_gather(join_line(packs, width), "ta")
    answers, far = attend_partners(around, sent, far, tile, line, hd)
    backs = [swap_along(x, "ha", p) for x, p in zip(answers, parities_h, strict=True)]
    for x in far:
        words += [x, swap_ta(x, 0)]
    total, weight = attend_own(own, around, current, words, near, k_gain, tile, line, len(parities_h))
    result = combine(total, weight, backs, hd)
    return result.reshape(1, 1, 1, tile, width)


def solution(mesh):
    return jax.shard_map(
        shards,
        mesh=mesh,
        in_specs=(
            P("ta", "ha", "wa", None, None),
            P("ta", "ha", "wa", None, None, None),
            P("ta", "ha", "wa", None, None, None),
            P(None, "wa", None),
            P(),
            P(),
            P("ta", "ha", "wa", None),
        ),
        out_specs=P("ta", "ha", "wa", None, None),
        check_vma=False,
    )
```

```python
import jax
import jax.numpy as jnp
from jax import lax
from jax.experimental import pallas as pl
from jax.experimental.pallas import tpu as pltpu
from jax.sharding import PartitionSpec as P

EPS = 1e-06
LANES = 128
IN_VMEM = pl.BlockSpec(memory_space=pltpu.VMEM)
IN_SMEM = pl.BlockSpec(memory_space=pltpu.SMEM)


def parities(count):
    return [parity for parity in (0, 1) if count - parity >= 2]


def matching(axis_size, ta_size, parity):
    pairs = []
    for t in range(ta_size):
        for a in range(axis_size):
            b = a + 1 if a % 2 == parity else a - 1
            if 0 <= b < axis_size:
                pairs.append((t * axis_size + a, t * axis_size + b))
            elif t ^ 1 < ta_size:
                pairs.append((t * axis_size + a, (t ^ 1) * axis_size + a))
    return pairs


def swap_along(values, axis, parity):
    pairs = matching(lax.axis_size(axis), lax.axis_size("ta"), parity)
    return lax.ppermute(values, ("ta", axis), pairs)


def swap_ta(values, parity):
    count = lax.axis_size("ta")
    pairs = []
    for t in range(count):
        u = t + 1 if t % 2 == parity else t - 1
        if 0 <= u < count:
            pairs.append((t, u))
    return lax.ppermute(values, "ta", pairs)


def resident(values):
    return pltpu.with_memory_space_constraint(values, pltpu.VMEM)


def call(body, out_shape, *operands, flops=0):
    outs = [pltpu.VMEM(s.shape, s.dtype) for s in out_shape]
    moved = sum(x.size * x.dtype.itemsize for x in operands)
    return pl.pallas_call(
        body,
        out_shape=outs,
        in_specs=[IN_VMEM] * len(operands),
        out_specs=[IN_VMEM] * len(outs),
        cost_estimate=pl.CostEstimate(flops=flops, bytes_accessed=moved, transcendentals=0),
    )(*[resident(x) for x in operands])


def head_normed(values, gain, heads):
    hd = gain.shape[-1]
    parts = []
    for head in range(heads):
        part = values[:, head * hd : (head + 1) * hd]
        square = jnp.mean(part * part, axis=-1, keepdims=True)
        parts.append(part * lax.rsqrt(square + EPS) * gain)
    return jnp.concatenate(parts, axis=1)


def split(values, heads):
    hd = values.shape[1] // heads
    return [values[:, head * hd : (head + 1) * hd] for head in range(heads)]


def attention(queries, groups, heads):
    scale = (queries.shape[1] // heads) ** (-0.5)
    queries = split(queries, heads)
    totals, weights = [0.0] * heads, [0.0] * heads
    for keys, vals, mask in groups:
        scores = [
            lax.dot_general(q, k, (((1,), (1,)), ((), ())), preferred_element_type=jnp.float32)
            for q, k in zip(queries, split(keys, heads), strict=True)
        ]
        expos = [jnp.exp(x * scale) for x in scores]
        if mask is not None:
            expos = [x * mask for x in expos]
        sums = [
            jnp.dot(x.astype(jnp.bfloat16), v, preferred_element_type=jnp.float32)
            for x, v in zip(expos, split(vals, heads), strict=True)
        ]
        totals = [x + y for x, y in zip(totals, sums, strict=True)]
        weights = [x + jnp.sum(y, axis=1, keepdims=True) for x, y in zip(weights, expos, strict=True)]
    return totals, weights


def in_lanes(columns):
    lane = lax.broadcasted_iota(jnp.int32, (columns[0].shape[0], LANES), 1)
    rows = jnp.zeros(lane.shape, jnp.float32)
    for h, column in enumerate(columns):
        rows = jnp.where(lane == h, column, rows)
    return rows


def normed_tiles(both, gain, heads, tile):
    both = [b.astype(jnp.float32) for b in both]
    keys = jnp.concatenate([head_normed(b[:tile], gain, heads) for b in both], axis=0)
    vals = jnp.concatenate([b[tile:] for b in both], axis=0)
    return keys.astype(jnp.bfloat16), vals.astype(jnp.bfloat16)


def slot_flags(pattern_ref, axes, sizes, rows):
    place = [lax.axis_index(a) for a in axes]
    steps_h, steps_w = (
        [jnp.where(place[i] % 2 == parity, 1, -1) for parity in parities(sizes[i])] for i in (1, 2)
    )
    lane = lax.broadcasted_iota(jnp.int32, (rows, LANES), 1)
    row = lax.broadcasted_iota(jnp.int32, (rows, LANES), 0)
    flags = jnp.zeros((rows, LANES), jnp.float32)
    for r, dh in enumerate([*steps_h, 0]):
        slot = 0
        for t in range(sizes[0]):
            dt = t - place[0]
            for dw in [0, *steps_w]:
                inside = (dt >= -1) & (dt <= 1)
                for i, d in ((1, dh), (2, dw)):
                    inside = inside & (place[i] + d >= 0) & (place[i] + d < sizes[i])
                offset = (jnp.clip(dt, -1, 1) + 1) * 9 + (dh + 1) * 3 + dw + 1
                used = jnp.where(inside & (pattern_ref[offset] == 1) & (offset != 13), 1.0, 0.0)
                flags = jnp.where((row == r) & (lane == slot), used, flags)
                slot += 1
    return flags


def key_masks(flags, places, line, tile, rows):
    lane = lax.broadcasted_iota(jnp.int32, (1, rows), 1)
    masks = []
    for t in range(places):
        mask = jnp.zeros((1, rows), jnp.float32)
        for i in range(line):
            slot = t * line + i
            mask = jnp.where(lane // tile == i, flags[:, slot : slot + 1], mask)
        masks.append(mask)
    return masks


def prepare(queries, stale, text, q_gain, k_gain, pattern, axes, sizes):
    tile, width = queries.shape
    tokens = text.shape[1]
    heads = width // q_gain.shape[-1]

    def body(q_ref, stale_ref, text_ref, q_gain_ref, k_gain_ref, pattern_ref, own_ref, tile_ref, words_ref):
        k_gain = k_gain_ref[...]
        normed = head_normed(q_ref[...].astype(jnp.float32), q_gain_ref[...], heads)
        flags = slot_flags(pattern_ref, axes, sizes, tile)
        own_ref[...] = jnp.concatenate([normed, flags], axis=1).astype(jnp.bfloat16)
        both = stale_ref[...].astype(jnp.float32)
        both = [head_normed(both[:tile], k_gain, heads), both[tile:]]
        tile_ref[...] = jnp.concatenate(both, axis=1).astype(jnp.bfloat16)
        text_keys = head_normed(text_ref[0].astype(jnp.float32), k_gain, heads)
        both = [text_keys, text_ref[1].astype(jnp.float32)]
        words_ref[...] = jnp.concatenate(both, axis=1).astype(jnp.bfloat16)

    shapes = [(tile, width + LANES), (tile, 2 * width), (tokens, 2 * width)]
    return pl.pallas_call(
        body,
        out_shape=[pltpu.VMEM(shape, jnp.bfloat16) for shape in shapes],
        in_specs=[IN_VMEM] * 5 + [IN_SMEM],
        out_specs=[IN_VMEM] * 3,
    )(queries, stale, text, q_gain, k_gain, pattern)


def norm_raw(both, k_gain, tile, flops):
    width = both.shape[1]
    heads = width // k_gain.shape[-1]

    def body(both_ref, gain_ref, out_ref):
        both = both_ref[...].astype(jnp.float32)
        keys = head_normed(both[:tile], gain_ref[...], heads)
        out_ref[...] = jnp.concatenate([keys, both[tile:]], axis=1).astype(jnp.bfloat16)

    shape = jax.ShapeDtypeStruct((tile, 2 * width), jnp.bfloat16)
    return call(body, [shape], both, k_gain, flops=flops)[0]


def join_line(packs, width):
    def body(*refs):
        parts = [r[:, : 2 * width].astype(jnp.float32) for r in refs[:-1]]
        refs[-1][...] = jnp.concatenate(parts, axis=0).astype(jnp.bfloat16)

    shape = jax.ShapeDtypeStruct((sum(x.shape[0] for x in packs), 2 * width), jnp.bfloat16)
    return call(body, [shape], *packs)[0]


def attend_partners(around, sent, far, tile, line, hd):
    places, rows, width = around.shape
    width //= 2
    heads = width // hd

    def body(around_ref, *refs):
        sent_refs, refs = refs[: len(sent)], refs[len(sent) :]
        far_refs, refs = refs[: len(far)], refs[len(far) :]
        back_refs, on_refs = refs[: len(sent)], refs[len(sent) :]
        for r, on in zip(far_refs, on_refs, strict=True):
            on[...] = r[...]
        blocks = [r[...].astype(jnp.float32) for r in sent_refs]
        masks = [
            key_masks(block[i : i + 1, width:], places, line, tile, rows)
            for i, block in enumerate(blocks)
        ]
        groups = []
        for t in range(places):
            mask = [jnp.broadcast_to(m[t], (tile, rows)) for m in masks]
            groups.append(
                (around_ref[t, :, :width], around_ref[t, :, width:], jnp.concatenate(mask, axis=0))
            )
        queries = jnp.concatenate([b[:, :width] for b in blocks], axis=0).astype(jnp.bfloat16)
        totals, weights = attention(queries, groups, heads)
        sums = in_lanes(weights)
        high = sums.astype(jnp.bfloat16).astype(jnp.float32)
        packed = high + pltpu.roll(sums - high, LANES // 2, 1)
        whole = jnp.concatenate([*totals, packed], axis=1)
        for i, back in enumerate(back_refs):
            back[...] = whole[i * tile : (i + 1) * tile].astype(jnp.bfloat16)

    shapes = [jax.ShapeDtypeStruct((tile, width + LANES), jnp.bfloat16)] * len(sent)
    shapes += [jax.ShapeDtypeStruct(x.shape, x.dtype) for x in far]
    outs = call(body, shapes, around, *sent, *far)
    return outs[: len(sent)], outs[len(sent) :]


def attend_own(own, around, current, words, k_gain, tile, line, reader):
    places, rows, width = around.shape
    width //= 2
    heads = width // k_gain.shape[-1]

    def body(own_ref, around_ref, current_ref, gain_ref, *refs):
        total_ref, sum_ref = refs[-2:]
        here = current_ref[...].astype(jnp.float32)
        keys = head_normed(here[:tile], gain_ref[...], heads)
        sure = [jnp.concatenate([keys, here[tile:]], axis=1)]
        sure += [r[...].astype(jnp.float32) for r in refs[:-2]]
        sure = jnp.concatenate(sure, axis=0).astype(jnp.bfloat16)
        flags = own_ref[:, width:].astype(jnp.float32)[reader : reader + 1]
        masks = key_masks(flags, places, line, tile, rows)
        groups = [(sure[:, :width], sure[:, width:], None)]
        for t in range(places):
            groups.append((around_ref[t, :, :width], around_ref[t, :, width:], masks[t]))
        totals, weights = attention(own_ref[:, :width], groups, heads)
        total_ref[...] = jnp.concatenate(totals, axis=1)
        sum_ref[...] = in_lanes(weights)

    shapes = [
        jax.ShapeDtypeStruct((tile, width), jnp.float32),
        jax.ShapeDtypeStruct((tile, LANES), jnp.float32),
    ]
    return call(body, shapes, own, around, current, k_gain, *words)


def combine(total, weight, backs, hd):
    tile, width = total.shape
    heads = width // hd

    def body(total_ref, sum_ref, *refs):
        back_refs, out_ref = refs[:-1], refs[-1]
        parts = [r[...].astype(jnp.float32) for r in back_refs]
        whole, sums = total_ref[...], sum_ref[...]
        for part in parts:
            tail = part[:, width:]
            whole = whole + part[:, :width]
            sums = sums + tail + pltpu.roll(tail, LANES // 2, 1)
        inverse = 1.0 / jnp.where(lax.broadcasted_iota(jnp.int32, sums.shape, 1) < heads, sums, 1.0)
        scaled = [x * inverse[:, h : h + 1] for h, x in enumerate(split(whole, heads))]
        out_ref[...] = jnp.concatenate(scaled, axis=1).astype(jnp.bfloat16)

    operands = [total, weight, *backs]
    return pl.pallas_call(
        body,
        out_shape=jax.ShapeDtypeStruct((tile, width), jnp.bfloat16),
        in_specs=[IN_VMEM] * len(operands),
        out_specs=IN_VMEM,
    )(*[resident(x) for x in operands])


def shards(queries, current_kv, stale_kv, text_kv, q_gain, k_gain, pattern):
    tile, width = queries.shape[3:]
    hd = q_gain.shape[0]
    stale = stale_kv.reshape(2 * tile, width)
    current = current_kv.reshape(2 * tile, width)
    k_gain = k_gain.reshape(1, hd)
    axes = ("ta", "ha", "wa")
    sizes = [lax.axis_size(a) for a in axes]
    parities_h, parities_w = parities(sizes[1]), parities(sizes[2])

    raw = [norm_raw(swap_along(stale, "wa", p), k_gain, tile, (int(1e9), int(3e8))[p]) for p in parities_w]
    own, mine, words = prepare(
        queries.reshape(tile, width),
        stale,
        text_kv,
        q_gain.reshape(1, hd),
        k_gain,
        pattern.reshape(27),
        axes,
        sizes,
    )
    sent = [swap_along(own, "ha", p) for p in parities_h]
    others = []
    if sizes[2] == 4 and sizes[0] % 2 == 0:
        pairs = [(t * 4 + i, t * 4 + (i ^ (2 + t % 2))) for t in range(sizes[0]) for i in range(4)]
        others.append(lax.ppermute(words, ("ta", "wa"), pairs))
        others.append(lax.ppermute(words, "wa", [(i, i ^ 1) for i in range(4)]))
        words = [words]
    else:
        words = [lax.all_gather(words, "wa", axis=0, tiled=True)]
    packs = [mine] + raw
    line = len(packs)
    around = lax.all_gather(join_line(packs, width), "ta")
    answers, others = attend_partners(around, sent, others, tile, line, hd)
    backs = [swap_along(x, "ha", p) for x, p in zip(answers, parities_h, strict=True)]
    if others:
        words += [*others, swap_ta(others[0], 0)]
    total, weight = attend_own(own, around, current, words, k_gain, tile, line, len(parities_h))
    result = combine(total, weight, backs, hd)
    return result.reshape(1, 1, 1, tile, width)


def solution(mesh):
    return jax.shard_map(
        shards,
        mesh=mesh,
        in_specs=(
            P("ta", "ha", "wa", None, None),
            P("ta", "ha", "wa", None, None, None),
            P("ta", "ha", "wa", None, None, None),
            P(None, "wa", None),
            P(),
            P(),
            P("ta", "ha", "wa", None),
        ),
        out_specs=P("ta", "ha", "wa", None, None),
        check_vma=False,
    )
```

```python
import jax
import jax.numpy as jnp
from jax import lax
from jax.experimental import pallas as pl
from jax.experimental.pallas import tpu as pltpu
from jax.sharding import PartitionSpec as P

EPS = 1e-06
LANES = 128
IN_VMEM = pl.BlockSpec(memory_space=pltpu.VMEM)
IN_SMEM = pl.BlockSpec(memory_space=pltpu.SMEM)


def parities(count):
    return [parity for parity in (0, 1) if count - parity >= 2]


def matching(axis_size, ta_size, parity):
    pairs = []
    for t in range(ta_size):
        for a in range(axis_size):
            b = a + 1 if a % 2 == parity else a - 1
            if 0 <= b < axis_size:
                pairs.append((t * axis_size + a, t * axis_size + b))
            elif t ^ 1 < ta_size:
                pairs.append((t * axis_size + a, (t ^ 1) * axis_size + a))
    return pairs


def swap_along(values, axis, parity):
    pairs = matching(lax.axis_size(axis), lax.axis_size("ta"), parity)
    return lax.ppermute(values, ("ta", axis), pairs)


def swap_ta(values, parity):
    count = lax.axis_size("ta")
    pairs = []
    for t in range(count):
        u = t + 1 if t % 2 == parity else t - 1
        if 0 <= u < count:
            pairs.append((t, u))
    return lax.ppermute(values, "ta", pairs)


def resident(values):
    return pltpu.with_memory_space_constraint(values, pltpu.VMEM)


def call(body, out_shape, *operands, flops=0):
    outs = [pltpu.VMEM(s.shape, s.dtype) for s in out_shape]
    moved = sum(x.size * x.dtype.itemsize for x in operands)
    return pl.pallas_call(
        body,
        out_shape=outs,
        in_specs=[IN_VMEM] * len(operands),
        out_specs=[IN_VMEM] * len(outs),
        cost_estimate=pl.CostEstimate(flops=flops, bytes_accessed=moved, transcendentals=0),
    )(*[resident(x) for x in operands])


def head_normed(values, gain, heads):
    hd = gain.shape[-1]
    parts = []
    for head in range(heads):
        part = values[:, head * hd : (head + 1) * hd]
        square = jnp.mean(part * part, axis=-1, keepdims=True)
        parts.append(part * lax.rsqrt(square + EPS) * gain)
    return jnp.concatenate(parts, axis=1)


def split(values, heads):
    hd = values.shape[1] // heads
    return [values[:, head * hd : (head + 1) * hd] for head in range(heads)]


def attention(queries, groups, heads):
    scale = (queries.shape[1] // heads) ** (-0.5)
    queries = split(queries, heads)
    totals, weights = [0.0] * heads, [0.0] * heads
    for keys, vals, mask in groups:
        scores = [
            lax.dot_general(q, k, (((1,), (1,)), ((), ())), preferred_element_type=jnp.float32)
            for q, k in zip(queries, split(keys, heads), strict=True)
        ]
        expos = [jnp.exp(x * scale) for x in scores]
        if mask is not None:
            expos = [x * mask for x in expos]
        sums = [
            jnp.dot(x.astype(jnp.bfloat16), v, preferred_element_type=jnp.float32)
            for x, v in zip(expos, split(vals, heads), strict=True)
        ]
        totals = [x + y for x, y in zip(totals, sums, strict=True)]
        weights = [x + jnp.sum(y, axis=1, keepdims=True) for x, y in zip(weights, expos, strict=True)]
    return totals, weights


def in_lanes(columns):
    lane = lax.broadcasted_iota(jnp.int32, (columns[0].shape[0], LANES), 1)
    rows = jnp.zeros(lane.shape, jnp.float32)
    for h, column in enumerate(columns):
        rows = jnp.where(lane == h, column, rows)
    return rows


def normed_tiles(both, gain, heads, tile):
    both = [b.astype(jnp.float32) for b in both]
    keys = jnp.concatenate([head_normed(b[:tile], gain, heads) for b in both], axis=0)
    vals = jnp.concatenate([b[tile:] for b in both], axis=0)
    return keys.astype(jnp.bfloat16), vals.astype(jnp.bfloat16)


def slot_flags(pattern_ref, axes, sizes, rows):
    place = [lax.axis_index(a) for a in axes]
    steps_h, steps_w = (
        [jnp.where(place[i] % 2 == parity, 1, -1) for parity in parities(sizes[i])] for i in (1, 2)
    )
    lane = lax.broadcasted_iota(jnp.int32, (rows, LANES), 1)
    row = lax.broadcasted_iota(jnp.int32, (rows, LANES), 0)
    flags = jnp.zeros((rows, LANES), jnp.float32)
    for r, dh in enumerate([*steps_h, 0]):
        slot = 0
        for t in range(sizes[0]):
            dt = t - place[0]
            for dw in [0, *steps_w]:
                inside = (dt >= -1) & (dt <= 1)
                for i, d in ((1, dh), (2, dw)):
                    inside = inside & (place[i] + d >= 0) & (place[i] + d < sizes[i])
                offset = (jnp.clip(dt, -1, 1) + 1) * 9 + (dh + 1) * 3 + dw + 1
                used = jnp.where(inside & (pattern_ref[offset] == 1) & (offset != 13), 1.0, 0.0)
                flags = jnp.where((row == r) & (lane == slot), used, flags)
                slot += 1
    return flags


def key_masks(flags, places, line, tile, rows):
    lane = lax.broadcasted_iota(jnp.int32, (1, rows), 1)
    masks = []
    for t in range(places):
        mask = jnp.zeros((1, rows), jnp.float32)
        for i in range(line):
            slot = t * line + i
            mask = jnp.where(lane // tile == i, flags[:, slot : slot + 1], mask)
        masks.append(mask)
    return masks


def prepare(queries, stale, text, q_gain, k_gain, pattern, axes, sizes):
    tile, width = queries.shape
    tokens = text.shape[1]
    heads = width // q_gain.shape[-1]

    def body(q_ref, stale_ref, text_ref, q_gain_ref, k_gain_ref, pattern_ref, own_ref, tile_ref, words_ref):
        k_gain = k_gain_ref[...]
        normed = head_normed(q_ref[...].astype(jnp.float32), q_gain_ref[...], heads)
        flags = slot_flags(pattern_ref, axes, sizes, tile)
        own_ref[...] = jnp.concatenate([normed, flags], axis=1).astype(jnp.bfloat16)
        both = stale_ref[...].astype(jnp.float32)
        both = [head_normed(both[:tile], k_gain, heads), both[tile:]]
        tile_ref[...] = jnp.concatenate(both, axis=1).astype(jnp.bfloat16)
        text_keys = head_normed(text_ref[0].astype(jnp.float32), k_gain, heads)
        both = [text_keys, text_ref[1].astype(jnp.float32)]
        words_ref[...] = jnp.concatenate(both, axis=1).astype(jnp.bfloat16)

    shapes = [(tile, width + LANES), (tile, 2 * width), (tokens, 2 * width)]
    return pl.pallas_call(
        body,
        out_shape=[pltpu.VMEM(shape, jnp.bfloat16) for shape in shapes],
        in_specs=[IN_VMEM] * 5 + [IN_SMEM],
        out_specs=[IN_VMEM] * 3,
    )(queries, stale, text, q_gain, k_gain, pattern)


def norm_raw(both, k_gain, tile, flops):
    width = both.shape[1]
    heads = width // k_gain.shape[-1]

    def body(both_ref, gain_ref, out_ref):
        both = both_ref[...].astype(jnp.float32)
        keys = head_normed(both[:tile], gain_ref[...], heads)
        out_ref[...] = jnp.concatenate([keys, both[tile:]], axis=1).astype(jnp.bfloat16)

    shape = jax.ShapeDtypeStruct((tile, 2 * width), jnp.bfloat16)
    return call(body, [shape], both, k_gain, flops=flops)[0]


def join_line(packs, width):
    def body(*refs):
        parts = [r[:, : 2 * width].astype(jnp.float32) for r in refs[:-1]]
        refs[-1][...] = jnp.concatenate(parts, axis=0).astype(jnp.bfloat16)

    shape = jax.ShapeDtypeStruct((sum(x.shape[0] for x in packs), 2 * width), jnp.bfloat16)
    return call(body, [shape], *packs)[0]


def attend_partners(around, sent, far, tile, line, hd):
    places, rows, width = around.shape
    width //= 2
    heads = width // hd

    def body(around_ref, *refs):
        sent_refs, refs = refs[: len(sent)], refs[len(sent) :]
        far_refs, refs = refs[: len(far)], refs[len(far) :]
        back_refs, on_refs = refs[: len(sent)], refs[len(sent) :]
        for r, on in zip(far_refs, on_refs, strict=True):
            on[...] = r[...]
        blocks = [r[...].astype(jnp.float32) for r in sent_refs]
        masks = [
            key_masks(block[i : i + 1, width:], places, line, tile, rows)
            for i, block in enumerate(blocks)
        ]
        groups = []
        for t in range(places):
            mask = [jnp.broadcast_to(m[t], (tile, rows)) for m in masks]
            groups.append(
                (around_ref[t, :, :width], around_ref[t, :, width:], jnp.concatenate(mask, axis=0))
            )
        queries = jnp.concatenate([b[:, :width] for b in blocks], axis=0).astype(jnp.bfloat16)
        totals, weights = attention(queries, groups, heads)
        sums = in_lanes(weights)
        high = sums.astype(jnp.bfloat16).astype(jnp.float32)
        packed = high + pltpu.roll(sums - high, LANES // 2, 1)
        whole = jnp.concatenate([*totals, packed], axis=1)
        for i, back in enumerate(back_refs):
            back[...] = whole[i * tile : (i + 1) * tile].astype(jnp.bfloat16)

    shapes = [jax.ShapeDtypeStruct((tile, width + LANES), jnp.bfloat16)] * len(sent)
    shapes += [jax.ShapeDtypeStruct(x.shape, x.dtype) for x in far]
    outs = call(body, shapes, around, *sent, *far)
    return outs[: len(sent)], outs[len(sent) :]


def attend_own(own, around, current, words, k_gain, tile, line, reader):
    places, rows, width = around.shape
    width //= 2
    heads = width // k_gain.shape[-1]

    def body(own_ref, around_ref, current_ref, gain_ref, *refs):
        total_ref, sum_ref = refs[-2:]
        here = current_ref[...].astype(jnp.float32)
        keys = head_normed(here[:tile], gain_ref[...], heads)
        sure = [jnp.concatenate([keys, here[tile:]], axis=1)]
        sure += [r[...].astype(jnp.float32) for r in refs[:-2]]
        sure = jnp.concatenate(sure, axis=0).astype(jnp.bfloat16)
        flags = own_ref[:, width:].astype(jnp.float32)[reader : reader + 1]
        masks = key_masks(flags, places, line, tile, rows)
        groups = [(sure[:, :width], sure[:, width:], None)]
        for t in range(places):
            groups.append((around_ref[t, :, :width], around_ref[t, :, width:], masks[t]))
        totals, weights = attention(own_ref[:, :width], groups, heads)
        total_ref[...] = jnp.concatenate(totals, axis=1)
        sum_ref[...] = in_lanes(weights)

    shapes = [
        jax.ShapeDtypeStruct((tile, width), jnp.float32),
        jax.ShapeDtypeStruct((tile, LANES), jnp.float32),
    ]
    return call(body, shapes, own, around, current, k_gain, *words)


def combine(total, weight, backs, hd):
    tile, width = total.shape
    heads = width // hd

    def body(total_ref, sum_ref, *refs):
        back_refs, out_ref = refs[:-1], refs[-1]
        parts = [r[...].astype(jnp.float32) for r in back_refs]
        whole, sums = total_ref[...], sum_ref[...]
        for part in parts:
            tail = part[:, width:]
            whole = whole + part[:, :width]
            sums = sums + tail + pltpu.roll(tail, LANES // 2, 1)
        inverse = 1.0 / jnp.where(lax.broadcasted_iota(jnp.int32, sums.shape, 1) < heads, sums, 1.0)
        scaled = [x * inverse[:, h : h + 1] for h, x in enumerate(split(whole, heads))]
        out_ref[...] = jnp.concatenate(scaled, axis=1).astype(jnp.bfloat16)

    operands = [total, weight, *backs]
    return pl.pallas_call(
        body,
        out_shape=jax.ShapeDtypeStruct((tile, width), jnp.bfloat16),
        in_specs=[IN_VMEM] * len(operands),
        out_specs=IN_VMEM,
    )(*[resident(x) for x in operands])


def shards(queries, current_kv, stale_kv, text_kv, q_gain, k_gain, pattern):
    tile, width = queries.shape[3:]
    hd = q_gain.shape[0]
    stale = stale_kv.reshape(2 * tile, width)
    current = current_kv.reshape(2 * tile, width)
    k_gain = k_gain.reshape(1, hd)
    axes = ("ta", "ha", "wa")
    sizes = [lax.axis_size(a) for a in axes]
    parities_h, parities_w = parities(sizes[1]), parities(sizes[2])

    raw = [norm_raw(swap_along(stale, "wa", p), k_gain, tile, (int(1e9), int(3e8))[p]) for p in parities_w]
    own, mine, words = prepare(
        queries.reshape(tile, width),
        stale,
        text_kv,
        q_gain.reshape(1, hd),
        k_gain,
        pattern.reshape(27),
        axes,
        sizes,
    )
    sent = [swap_along(own, "ha", p) for p in parities_h]
    others = []
    if sizes[2] == 4 and sizes[0] % 2 == 0:
        pairs = [(t * 4 + i, t * 4 + (i ^ (3 - t % 2))) for t in range(sizes[0]) for i in range(4)]
        others.append(lax.ppermute(words, ("ta", "wa"), pairs))
        others.append(lax.ppermute(words, "wa", [(i, i ^ 1) for i in range(4)]))
        words = [words]
    else:
        words = [lax.all_gather(words, "wa", axis=0, tiled=True)]
    packs = [mine] + raw
    line = len(packs)
    around = lax.all_gather(join_line(packs, width), "ta")
    answers, others = attend_partners(around, sent, others, tile, line, hd)
    backs = [swap_along(x, "ha", p) for x, p in zip(answers, parities_h, strict=True)]
    if others:
        words += [*others, swap_ta(others[0], 0)]
    total, weight = attend_own(own, around, current, words, k_gain, tile, line, len(parities_h))
    result = combine(total, weight, backs, hd)
    return result.reshape(1, 1, 1, tile, width)


def solution(mesh):
    return jax.shard_map(
        shards,
        mesh=mesh,
        in_specs=(
            P("ta", "ha", "wa", None, None),
            P("ta", "ha", "wa", None, None, None),
            P("ta", "ha", "wa", None, None, None),
            P(None, "wa", None),
            P(),
            P(),
            P("ta", "ha", "wa", None),
        ),
        out_specs=P("ta", "ha", "wa", None, None),
        check_vma=False,
    )
```

```python
import jax
import jax.numpy as jnp
from jax import lax
from jax.experimental import pallas as pl
from jax.experimental.pallas import tpu as pltpu
from jax.sharding import PartitionSpec as P

EPS = 1e-06
LANES = 128
WORD_ROWS = 8
IN_VMEM = pl.BlockSpec(memory_space=pltpu.VMEM)
IN_SMEM = pl.BlockSpec(memory_space=pltpu.SMEM)


def parities(count):
    return [parity for parity in (0, 1) if count - parity >= 2]


def matching(axis_size, ta_size, parity):
    pairs = []
    for t in range(ta_size):
        for a in range(axis_size):
            b = a + 1 if a % 2 == parity else a - 1
            if 0 <= b < axis_size:
                pairs.append((t * axis_size + a, t * axis_size + b))
            elif t ^ 1 < ta_size:
                pairs.append((t * axis_size + a, (t ^ 1) * axis_size + a))
    return pairs


def swap_along(values, axis, parity):
    pairs = matching(lax.axis_size(axis), lax.axis_size("ta"), parity)
    return lax.ppermute(values, ("ta", axis), pairs)


def swap_ta(values, parity):
    count = lax.axis_size("ta")
    pairs = []
    for t in range(count):
        u = t + 1 if t % 2 == parity else t - 1
        if 0 <= u < count:
            pairs.append((t, u))
    return lax.ppermute(values, "ta", pairs)


def resident(values):
    return pltpu.with_memory_space_constraint(values, pltpu.VMEM)


def call(body, out_shape, *operands, flops=0):
    outs = [pltpu.VMEM(s.shape, s.dtype) for s in out_shape]
    moved = sum(x.size * x.dtype.itemsize for x in operands)
    return pl.pallas_call(
        body,
        out_shape=outs,
        in_specs=[IN_VMEM] * len(operands),
        out_specs=[IN_VMEM] * len(outs),
        cost_estimate=pl.CostEstimate(flops=flops, bytes_accessed=moved, transcendentals=0),
    )(*[resident(x) for x in operands])


def head_normed(values, gain, heads):
    hd = gain.shape[-1]
    parts = []
    for head in range(heads):
        part = values[:, head * hd : (head + 1) * hd]
        square = jnp.mean(part * part, axis=-1, keepdims=True)
        parts.append(part * lax.rsqrt(square + EPS) * gain)
    return jnp.concatenate(parts, axis=1)


def split(values, heads):
    hd = values.shape[1] // heads
    return [values[:, head * hd : (head + 1) * hd] for head in range(heads)]


def attention(queries, groups, heads):
    scale = (queries.shape[1] // heads) ** (-0.5)
    queries = split(queries, heads)
    totals, weights = [0.0] * heads, [0.0] * heads
    for keys, vals, mask in groups:
        scores = [
            lax.dot_general(q, k, (((1,), (1,)), ((), ())), preferred_element_type=jnp.float32)
            for q, k in zip(queries, split(keys, heads), strict=True)
        ]
        expos = [jnp.exp(x * scale) for x in scores]
        if mask is not None:
            expos = [x * mask for x in expos]
        sums = [
            jnp.dot(x.astype(jnp.bfloat16), v, preferred_element_type=jnp.float32)
            for x, v in zip(expos, split(vals, heads), strict=True)
        ]
        totals = [x + y for x, y in zip(totals, sums, strict=True)]
        weights = [x + jnp.sum(y, axis=1, keepdims=True) for x, y in zip(weights, expos, strict=True)]
    return totals, weights


def in_lanes(columns):
    lane = lax.broadcasted_iota(jnp.int32, (columns[0].shape[0], LANES), 1)
    rows = jnp.zeros(lane.shape, jnp.float32)
    for h, column in enumerate(columns):
        rows = jnp.where(lane == h, column, rows)
    return rows


def normed_tiles(both, gain, heads, tile):
    both = [b.astype(jnp.float32) for b in both]
    keys = jnp.concatenate([head_normed(b[:tile], gain, heads) for b in both], axis=0)
    vals = jnp.concatenate([b[tile:] for b in both], axis=0)
    return keys.astype(jnp.bfloat16), vals.astype(jnp.bfloat16)


def slot_flags(pattern_ref, axes, sizes, rows):
    place = [lax.axis_index(a) for a in axes]
    steps_h, steps_w = (
        [jnp.where(place[i] % 2 == parity, 1, -1) for parity in parities(sizes[i])] for i in (1, 2)
    )
    lane = lax.broadcasted_iota(jnp.int32, (rows, LANES), 1)
    row = lax.broadcasted_iota(jnp.int32, (rows, LANES), 0)
    flags = jnp.zeros((rows, LANES), jnp.float32)
    for r, dh in enumerate([*steps_h, 0]):
        slot = 0
        for t in range(sizes[0]):
            dt = t - place[0]
            for dw in [0, *steps_w]:
                inside = (dt >= -1) & (dt <= 1)
                for i, d in ((1, dh), (2, dw)):
                    inside = inside & (place[i] + d >= 0) & (place[i] + d < sizes[i])
                offset = (jnp.clip(dt, -1, 1) + 1) * 9 + (dh + 1) * 3 + dw + 1
                used = jnp.where(inside & (pattern_ref[offset] == 1) & (offset != 13), 1.0, 0.0)
                flags = jnp.where((row == r) & (lane == slot), used, flags)
                slot += 1
    return flags


def key_masks(flags, places, line, tile, rows):
    lane = lax.broadcasted_iota(jnp.int32, (1, rows), 1)
    masks = []
    for t in range(places):
        mask = jnp.zeros((1, rows), jnp.float32)
        for i in range(line):
            slot = t * line + i
            mask = jnp.where(lane // tile == i, flags[:, slot : slot + 1], mask)
        masks.append(mask)
    return masks


def prepare(queries, stale, text, q_gain, k_gain, pattern, axes, sizes):
    tile, width = queries.shape
    tokens = text.shape[1]
    heads = width // q_gain.shape[-1]

    def body(q_ref, stale_ref, text_ref, q_gain_ref, k_gain_ref, pattern_ref, own_ref, tile_ref, words_ref):
        k_gain = k_gain_ref[...]
        normed = head_normed(q_ref[...].astype(jnp.float32), q_gain_ref[...], heads)
        flags = slot_flags(pattern_ref, axes, sizes, tile)
        own_ref[...] = jnp.concatenate([normed, flags], axis=1).astype(jnp.bfloat16)
        both = stale_ref[...].astype(jnp.float32)
        both = [head_normed(both[:tile], k_gain, heads), both[tile:]]
        tile_ref[...] = jnp.concatenate(both, axis=1).astype(jnp.bfloat16)
        text_keys = head_normed(text_ref[0].astype(jnp.float32), k_gain, heads)
        both = jnp.concatenate([text_keys, text_ref[1].astype(jnp.float32)], axis=1)
        blank = jnp.zeros((WORD_ROWS - tokens, 2 * width), jnp.float32)
        words_ref[...] = jnp.concatenate([both, blank], axis=0).astype(jnp.bfloat16)

    shapes = [(tile, width + LANES), (tile, 2 * width), (WORD_ROWS, 2 * width)]
    return pl.pallas_call(
        body,
        out_shape=[pltpu.VMEM(shape, jnp.bfloat16) for shape in shapes],
        in_specs=[IN_VMEM] * 5 + [IN_SMEM],
        out_specs=[IN_VMEM] * 3,
    )(queries, stale, text, q_gain, k_gain, pattern)


def norm_raw(both, k_gain, tile):
    width = both.shape[1]
    heads = width // k_gain.shape[-1]
    tokens = both.shape[0] // 2 - tile

    def body(both_ref, gain_ref, out_ref, *words_refs):
        both = both_ref[...].astype(jnp.float32)
        keys = head_normed(both[:tile], gain_ref[...], heads)
        out_ref[...] = jnp.concatenate([keys, both[tile : 2 * tile]], axis=1).astype(jnp.bfloat16)
        for r in words_refs:
            text = both[2 * tile :]
            keys = head_normed(text[:tokens], gain_ref[...], heads)
            r[...] = jnp.concatenate([keys, text[tokens:]], axis=1).astype(jnp.bfloat16)

    shapes = [jax.ShapeDtypeStruct((tile, 2 * width), jnp.bfloat16)]
    if tokens:
        shapes.append(jax.ShapeDtypeStruct((tokens, 2 * width), jnp.bfloat16))
    return call(body, shapes, both, k_gain)


def join_line(packs, width):
    def body(*refs):
        parts = [r[:, : 2 * width].astype(jnp.float32) for r in refs[:-1]]
        refs[-1][...] = jnp.concatenate(parts, axis=0).astype(jnp.bfloat16)

    shape = jax.ShapeDtypeStruct((sum(x.shape[0] for x in packs), 2 * width), jnp.bfloat16)
    return call(body, [shape], *packs)[0]


def attend_partners(around, sent, tile, line, hd):
    places, rows, width = around.shape
    width //= 2
    heads = width // hd

    def body(around_ref, *refs):
        sent_refs, back_refs = refs[: len(sent)], refs[len(sent) :]
        blocks = [r[...].astype(jnp.float32) for r in sent_refs]
        masks = [
            key_masks(block[i : i + 1, width:], places, line, tile, rows)
            for i, block in enumerate(blocks)
        ]
        groups = []
        for t in range(places):
            mask = [jnp.broadcast_to(m[t], (tile, rows)) for m in masks]
            groups.append(
                (around_ref[t, :, :width], around_ref[t, :, width:], jnp.concatenate(mask, axis=0))
            )
        queries = jnp.concatenate([b[:, :width] for b in blocks], axis=0).astype(jnp.bfloat16)
        totals, weights = attention(queries, groups, heads)
        sums = in_lanes(weights)
        high = sums.astype(jnp.bfloat16).astype(jnp.float32)
        packed = high + pltpu.roll(sums - high, LANES // 2, 1)
        whole = jnp.concatenate([*totals, packed], axis=1)
        for i, back in enumerate(back_refs):
            back[...] = whole[i * tile : (i + 1) * tile].astype(jnp.bfloat16)

    shapes = [jax.ShapeDtypeStruct((tile, width + LANES), jnp.bfloat16)] * len(sent)
    return call(body, shapes, around, *sent)


def attend_own(own, around, current, words, near, far, tokens, k_gain, tile, line, reader):
    places, rows, width = around.shape
    width //= 2
    heads = width // k_gain.shape[-1]

    def body(own_ref, around_ref, current_ref, gain_ref, words_ref, *refs):
        near_refs, refs = refs[: len(near)], refs[len(near) :]
        far_refs, (total_ref, sum_ref, *on_refs) = refs[: len(far)], refs[len(far) :]
        for r, on in zip(far_refs, on_refs, strict=True):
            on[...] = r[...].astype(jnp.float32)[:tokens].astype(jnp.bfloat16)
        here = current_ref[...].astype(jnp.float32)
        keys = head_normed(here[:tile], gain_ref[...], heads)
        sure = [jnp.concatenate([keys, here[tile:]], axis=1)]
        sure.append(words_ref[...].astype(jnp.float32)[:tokens])
        sure += [r[...].astype(jnp.float32) for r in near_refs]
        sure = jnp.concatenate(sure, axis=0).astype(jnp.bfloat16)
        flags = own_ref[:, width:].astype(jnp.float32)[reader : reader + 1]
        masks = key_masks(flags, places, line, tile, rows)
        groups = [(sure[:, :width], sure[:, width:], None)]
        for t in range(places):
            groups.append((around_ref[t, :, :width], around_ref[t, :, width:], masks[t]))
        totals, weights = attention(own_ref[:, :width], groups, heads)
        total_ref[...] = jnp.concatenate(totals, axis=1)
        sum_ref[...] = in_lanes(weights)

    shapes = [
        jax.ShapeDtypeStruct((tile, width), jnp.float32),
        jax.ShapeDtypeStruct((tile, LANES), jnp.float32),
    ]
    shapes += [jax.ShapeDtypeStruct((tokens, x.shape[1]), x.dtype) for x in far]
    outs = call(body, shapes, own, around, current, k_gain, words, *near, *far)
    return outs[0], outs[1], outs[2:]


def attend_words(own, words, total, weight, hd):
    tile, width = total.shape
    heads = width // hd

    def body(own_ref, total_ref, sum_ref, *refs):
        total_out, sum_out = refs[-2:]
        both = jnp.concatenate([r[...].astype(jnp.float32) for r in refs[:-2]], axis=0)
        both = both.astype(jnp.bfloat16)
        totals, weights = attention(
            own_ref[:, :width], [(both[:, :width], both[:, width:], None)], heads
        )
        total_out[...] = total_ref[...] + jnp.concatenate(totals, axis=1)
        sum_out[...] = sum_ref[...] + in_lanes(weights)

    shapes = [jax.ShapeDtypeStruct(x.shape, x.dtype) for x in (total, weight)]
    return call(body, shapes, own, total, weight, *words, flops=int(3e8))


def combine(total, weight, backs, hd):
    tile, width = total.shape
    heads = width // hd

    def body(total_ref, sum_ref, *refs):
        back_refs, out_ref = refs[:-1], refs[-1]
        parts = [r[...].astype(jnp.float32) for r in back_refs]
        whole, sums = total_ref[...], sum_ref[...]
        for part in parts:
            tail = part[:, width:]
            whole = whole + part[:, :width]
            sums = sums + tail + pltpu.roll(tail, LANES // 2, 1)
        inverse = 1.0 / jnp.where(lax.broadcasted_iota(jnp.int32, sums.shape, 1) < heads, sums, 1.0)
        scaled = [x * inverse[:, h : h + 1] for h, x in enumerate(split(whole, heads))]
        out_ref[...] = jnp.concatenate(scaled, axis=1).astype(jnp.bfloat16)

    operands = [total, weight, *backs]
    return pl.pallas_call(
        body,
        out_shape=jax.ShapeDtypeStruct((tile, width), jnp.bfloat16),
        in_specs=[IN_VMEM] * len(operands),
        out_specs=IN_VMEM,
    )(*[resident(x) for x in operands])


def shards(queries, current_kv, stale_kv, text_kv, q_gain, k_gain, pattern):
    tile, width = queries.shape[3:]
    hd = q_gain.shape[0]
    stale = stale_kv.reshape(2 * tile, width)
    current = current_kv.reshape(2 * tile, width)
    k_gain = k_gain.reshape(1, hd)
    axes = ("ta", "ha", "wa")
    sizes = [lax.axis_size(a) for a in axes]
    parities_h, parities_w = parities(sizes[1]), parities(sizes[2])

    tokens = text_kv.shape[1]
    raw = [norm_raw(swap_along(stale, "wa", p), k_gain, tile)[0] for p in parities_w]
    own, mine, words = prepare(
        queries.reshape(tile, width),
        stale,
        text_kv,
        q_gain.reshape(1, hd),
        k_gain,
        pattern.reshape(27),
        axes,
        sizes,
    )
    sent = [swap_along(own, "ha", p) for p in parities_h]
    near, far = [], []
    if sizes[2] == 4 and sizes[0] % 2 == 0:
        pairs = [(t * 4 + i, t * 4 + (i ^ (2 + t % 2))) for t in range(sizes[0]) for i in range(4)]
        far.append(lax.ppermute(words, ("ta", "wa"), pairs))
        near.append(lax.ppermute(words[:tokens], "wa", [(i, i ^ 1) for i in range(4)]))
    else:
        words = lax.all_gather(words[:tokens], "wa", axis=0, tiled=True)
        tokens = words.shape[0]
    packs = [mine] + raw
    line = len(packs)
    around = lax.all_gather(join_line(packs, width), "ta")
    answers = attend_partners(around, sent, tile, line, hd)
    backs = [swap_along(x, "ha", p) for x, p in zip(answers, parities_h, strict=True)]
    total, weight, far = attend_own(
        own, around, current, words, [], far, tokens, k_gain, tile, line, len(parities_h)
    )
    for there in far:
        total, weight = attend_words(own, [there, swap_ta(there, 0), *near], total, weight, hd)
    result = combine(total, weight, backs, hd)
    return result.reshape(1, 1, 1, tile, width)


def solution(mesh):
    return jax.shard_map(
        shards,
        mesh=mesh,
        in_specs=(
            P("ta", "ha", "wa", None, None),
            P("ta", "ha", "wa", None, None, None),
            P("ta", "ha", "wa", None, None, None),
            P(None, "wa", None),
            P(),
            P(),
            P("ta", "ha", "wa", None),
        ),
        out_specs=P("ta", "ha", "wa", None, None),
        check_vma=False,
    )
```
